128 devices in a mesh: req: 16 (over y, z), tp: 8 (over x, core).
Axes of the slice: x: 4, y: 4, z: 4, core: 2. Of those that a mesh axis runs over, the one named last changes fastest.
Arguments:
- hidden: bfloat16 [14336, 8192], P('req'), may hold values from -150 to 150
- norm_gain_vector: float32 [8192], replicated, may hold values from 0.1 to 1.9
- query_weight: bfloat16 [8192, 4096], P(None, 'tp'), may hold values from -0.0625 to 0.0625
- adapter_down_weight: bfloat16 [128, 64, 8192], P(('req', 'tp')), may hold values from -0.0625 to 0.0625
- adapter_up_weight: bfloat16 [128, 64, 4096], P(('req', 'tp')), may hold values from -0.75 to 0.75
- block_adapter_ids: int32 [16, 7], replicated, may hold values from 0 to 127, as said below
- adapter_slot_table: int32 [128], replicated, may hold values from 0 to 127, as said below
Outputs:
- query: bfloat16 [14336, 4096], P('req', 'tp')
The draws below stay inside these ranges and needn't reach their ends.
Inputs may be any that keep to these rules, and one draw needn't show every extreme that they name: `block_adapter_ids`: in every request group the 7 blocks use different adapters, and no two of them have storage slots s, s2 with s // 8 == s2 // 8. `adapter_slot_table`: each storage slot holds exactly one adapter id.
All inputs are finite; a program needn't handle non-finite values.
Results may differ from the reference program's by a relative error of at most 0.0052.
Values may be sent and summed in bfloat16 or wider, within the bound.
No kernel may reach another device: no remote copies, remote signals or barrier semaphores. Data moves between devices by JAX's collectives and lax.ppermute only.
A program may use at most 192 MiB of HBM per device.

```python
import math
import jax
import jax.numpy as jnp
from jax import lax

MODEL_WIDTH = 8192
QUERY_WIDTH = 4096
ADAPTER_RANK = 64
BLOCK = 128
NBLK = 7
TOKENS = 14336
ADAPTER_TOTAL = 128
N_REQ = 16
N_TP = 8


def shared_tables(key):
    first, second, third = jax.random.split(key, 3)
    owner = jax.random.permutation(first, ADAPTER_TOTAL).astype(jnp.int32)
    inverse = jnp.argsort(owner).astype(jnp.int32)
    group_keys = jax.random.split(second, N_REQ)
    columns = jax.vmap(lambda k: jax.random.permutation(k, N_REQ)[:NBLK])(group_keys)
    within = jax.random.randint(third, (N_REQ, NBLK), 0, N_TP)
    slots = (columns * N_TP + within).astype(jnp.int32)
    return (owner, inverse[slots])


def draw_adapter_slot_table(key, part):
    owner, ids = shared_tables(key)
    return owner


def draw_block_adapter_ids(key, part):
    owner, ids = shared_tables(key)
    return ids.astype(jnp.int32)


def draw_hidden(key, part):
    key = jax.random.fold_in(key, 3)
    first, second, third = jax.random.split(key, 3)
    row_scale = jnp.exp(jax.random.uniform(second, (TOKENS, 1), jnp.float32, 0.0, math.log(10.0)))
    col_scale = jnp.exp(jax.random.uniform(third, (1, MODEL_WIDTH), jnp.float32, math.log(0.3), math.log(3.0)))
    values = jnp.clip(jax.random.normal(first, (TOKENS, MODEL_WIDTH), jnp.float32), -4.5, 4.5)
    return (values * row_scale * col_scale).astype(jnp.bfloat16)


def block_scale(key, extent, cuts, low, top_value):
    def one(dim, parts):
        draws = jax.random.uniform(jax.random.fold_in(jax.random.fold_in(key, 6), dim), (parts,), jnp.float32, low / len(cuts), top_value / len(cuts))
        return jnp.repeat(jnp.exp(draws), extent[dim] // parts).reshape((-1,) + (1,) * (len(extent) - dim - 1))

    loudness = one(*cuts[0])
    for cut in cuts[1:]:
        loudness = loudness * one(*cut)
    return loudness


def noise(own_key, shape, width, most, shards=(), dtype=jnp.bfloat16):
    drawn = width * jax.random.normal(own_key, shape, jnp.float32)
    if shards:
        drawn = drawn * block_scale(own_key, shape, shards, -0.22, 0.18)
    return jnp.clip(drawn, -most, most).astype(dtype)


def setup_inputs(seed: int = 0) -> dict:
    key_of = jax.random.split(jax.random.key(seed), 8)
    return {
        "hidden": draw_hidden(jax.random.fold_in(key_of[7], 71), 0),
        "norm_gain_vector": jnp.clip(1.0 + 0.18 * jax.random.normal(key_of[1], (MODEL_WIDTH,), jnp.float32), 0.1, 1.9),
        "query_weight": noise(key_of[2], (MODEL_WIDTH, QUERY_WIDTH), MODEL_WIDTH ** -0.5, 0.0625, ((1, 8),)),
        "adapter_down_weight": noise(key_of[3], (ADAPTER_TOTAL, ADAPTER_RANK, MODEL_WIDTH), MODEL_WIDTH ** -0.5, 0.0625, ((0, 128),)),
        "adapter_up_weight": noise(key_of[4], (ADAPTER_TOTAL, ADAPTER_RANK, QUERY_WIDTH), ADAPTER_RANK ** -0.5, 0.75, ((0, 128),)),
        "block_adapter_ids": draw_block_adapter_ids(jax.random.fold_in(key_of[7], 71), 0),
        "adapter_slot_table": draw_adapter_slot_table(jax.random.fold_in(key_of[7], 71), 0),
    }


ADAPTER_SCALE = 0.5

def reference(hidden, norm_gain_vector, query_weight, adapter_down_weight, adapter_up_weight, block_adapter_ids, adapter_slot_table):
    slot_table = adapter_slot_table[block_adapter_ids]

    def one_group(item):
        rows, group_slot_ids = item
        wide = rows.astype(jnp.float32)
        inverse_rms = lax.rsqrt(lax.optimization_barrier(jnp.mean(wide * wide, axis=-1, keepdims=True)) + 1e-05)
        normed = (wide * inverse_rms * norm_gain_vector).astype(jnp.bfloat16)
        base_output = jnp.dot(normed, query_weight, preferred_element_type=jnp.float32)
        down_selected = adapter_down_weight[group_slot_ids].astype(jnp.float32)
        up_selected = adapter_up_weight[group_slot_ids].astype(jnp.float32)
        block_rows = normed.reshape(NBLK, BLOCK, MODEL_WIDTH).astype(jnp.float32)
        shrink = jnp.einsum('jrd,jbd->jrb', down_selected, block_rows).astype(jnp.bfloat16)
        rank_output = jnp.einsum('jrb,jrc->jbc', shrink.astype(jnp.float32), up_selected).reshape(NBLK * BLOCK, QUERY_WIDTH)
        return (base_output + ADAPTER_SCALE * rank_output).astype(jnp.bfloat16)
    result = lax.map(one_group, (hidden.reshape(N_REQ, NBLK * BLOCK, MODEL_WIDTH), slot_table))
    return result.reshape(N_REQ * NBLK * BLOCK, QUERY_WIDTH)
```

```python
import functools

import jax
import jax.numpy as jnp
from jax import lax
from jax.experimental import pallas as pl
from jax.experimental.pallas import tpu as pltpu
from jax.sharding import PartitionSpec as P

ADAPTER_SCALE = 0.5
X, CORES = 4, 2
LANES = X * CORES
BOTH = ("req", "tp")


def lane_shift(groups, dx, dc):
    return [
        (g * LANES + x * CORES + c, g * LANES + (x + dx) % X * CORES + (c + dc) % CORES)
        for g in range(groups)
        for x in range(X)
        for c in range(CORES)
    ]


def relative(lane, other):
    dx = (lane // CORES - other // CORES) % X
    dc = (lane % CORES - other % CORES) % CORES
    return dx * CORES + dc


def split_kernel(lane_ref, up_ref, *rest):
    outs, sems = rest[:LANES], rest[LANES]
    lane = lane_ref[0]
    width = outs[0].shape[1]
    copies = []
    for k in range(LANES):
        dx, dc = k // CORES, k % CORES
        to = (lane // CORES + dx) % X * CORES + (lane % CORES + dc) % CORES
        col = pl.multiple_of(to * width, width)
        copies.append(pltpu.make_async_copy(up_ref.at[0, :, pl.ds(col, width)], outs[k], sems.at[k]))
    for copy in copies:
        copy.start()
    for copy in copies:
        copy.wait()


def split_up(lane, up):
    rank, cols = up.shape[1:]
    width = cols // LANES
    any_spec = pl.BlockSpec(memory_space=pl.ANY)
    return pl.pallas_call(
        split_kernel,
        grid_spec=pltpu.PrefetchScalarGridSpec(
            num_scalar_prefetch=1,
            grid=(1,),
            in_specs=[any_spec],
            out_specs=[any_spec] * LANES,
            scratch_shapes=[pltpu.SemaphoreType.DMA((LANES,))],
        ),
        out_shape=[jax.ShapeDtypeStruct((rank, width), up.dtype)] * LANES,
        name="split_up",
    )(lane, up)


def pick_kernel(pick_ref, src_ref, out_ref, sems):
    copies = [
        pltpu.make_async_copy(src_ref.at[pick_ref[g]], out_ref.at[g], sems.at[g])
        for g in range(out_ref.shape[0])
    ]
    for copy in copies:
        copy.start()
    for copy in copies:
        copy.wait()


def pick_down(pick, pieces):
    any_spec = pl.BlockSpec(memory_space=pl.ANY)
    groups = pick.shape[0]
    return pl.pallas_call(
        pick_kernel,
        grid_spec=pltpu.PrefetchScalarGridSpec(
            num_scalar_prefetch=1,
            grid=(1,),
            in_specs=[any_spec],
            out_specs=any_spec,
            scratch_shapes=[pltpu.SemaphoreType.DMA((groups,))],
        ),
        out_shape=jax.ShapeDtypeStruct((groups,) + pieces.shape[1:], pieces.dtype),
        name="pick_down",
    )(pick, pieces)


def pick_many_kernel(pick_ref, *rest):
    srcs, out_ref, sems = rest[:LANES], rest[LANES], rest[LANES + 1]
    groups = out_ref.shape[0]
    for g in range(groups):
        for k in range(LANES):

            @pl.when(pick_ref[g] == k)
            def _():
                pltpu.make_async_copy(srcs[k], out_ref.at[g], sems.at[g]).start()

    for g in range(groups):
        pltpu.make_async_copy(srcs[0], out_ref.at[g], sems.at[g]).wait()


def pick_up(pick, pieces):
    any_spec = pl.BlockSpec(memory_space=pl.ANY)
    groups = pick.shape[0]
    return pl.pallas_call(
        pick_many_kernel,
        grid_spec=pltpu.PrefetchScalarGridSpec(
            num_scalar_prefetch=1,
            grid=(1,),
            in_specs=[any_spec] * LANES,
            out_specs=any_spec,
            scratch_shapes=[pltpu.SemaphoreType.DMA((groups,))],
        ),
        out_shape=jax.ShapeDtypeStruct((groups,) + pieces[0].shape, pieces[0].dtype),
        name="pick_up",
    )(pick, *pieces)


def shrink_kernel(row_ref, down_ref, normed_ref, low_ref):
    low_ref[0] = lax.dot_general(
        down_ref[0], normed_ref[...], (((1,), (1,)), ((), ())), preferred_element_type=jnp.float32
    )


def shrink(owner_rows, down_got, normed, blocks):
    rows, features = normed.shape
    block = rows // blocks
    part = down_got.shape[1]
    return pl.pallas_call(
        shrink_kernel,
        grid_spec=pltpu.PrefetchScalarGridSpec(
            num_scalar_prefetch=1,
            grid=(blocks,),
            in_specs=[
                pl.BlockSpec((1, part, features), lambda j, row: (row[j], 0, 0)),
                pl.BlockSpec((block, features), lambda j, row: (j, 0)),
            ],
            out_specs=pl.BlockSpec((1, part, block), lambda j, row: (j, 0, 0)),
        ),
        out_shape=jax.ShapeDtypeStruct((blocks, part, block), jnp.float32),
        compiler_params=pltpu.CompilerParams(vmem_limit_bytes=32 * 2**20),
        cost_estimate=pl.CostEstimate(
            flops=2 * rows * features * 256, bytes_accessed=2 * rows * features, transcendentals=0
        ),
        name="shrink",
    )(owner_rows, down_got, normed)


def expand_kernel(row_ref, lane_ref, base_ref, low0, low1, low2, low3, up_ref, out_ref, full):
    lows = (low0, low1, low2, low3)
    lane = lane_ref[0]
    part = low0.shape[2]
    for dx in range(X):
        for dc in range(CORES):
            src = (lane // CORES - dx) % X * CORES + (lane % CORES - dc) % CORES
            full[pl.ds(pl.multiple_of(src * part, part), part), :] = lows[dx][dc, 0]
    low = full[...].astype(jnp.bfloat16)
    term = lax.dot_general(low, up_ref[0], (((0,), (0,)), ((), ())), preferred_element_type=jnp.float32)
    out_ref[...] = (base_ref[...] + ADAPTER_SCALE * term).astype(out_ref.dtype)


def expand(owner_rows, lane, base, lows, up_got, blocks):
    rows, cols = base.shape
    block = rows // blocks
    part = lows[0].shape[2]
    rank = up_got.shape[1]
    low_spec = pl.BlockSpec((CORES, 1, part, block), lambda j, row, lane: (0, j, 0, 0))
    return pl.pallas_call(
        expand_kernel,
        grid_spec=pltpu.PrefetchScalarGridSpec(
            num_scalar_prefetch=2,
            grid=(blocks,),
            in_specs=[
                pl.BlockSpec((block, cols), lambda j, row, lane: (j, 0)),
                low_spec,
                low_spec,
                low_spec,
                low_spec,
                pl.BlockSpec((1, rank, cols), lambda j, row, lane: (row[j], 0, 0)),
            ],
            out_specs=pl.BlockSpec((block, cols), lambda j, row, lane: (j, 0)),
            scratch_shapes=[pltpu.VMEM((rank, block), jnp.float32)],
        ),
        out_shape=jax.ShapeDtypeStruct((rows, cols), jnp.bfloat16),
        name="expand",
    )(owner_rows, lane, base, *lows, up_got)


def shards(
    hidden,
    norm_gain_vector,
    query_weight,
    adapter_down_weight,
    adapter_up_weight,
    block_adapter_ids,
    adapter_slot_table,
):
    groups, blocks = block_adapter_ids.shape
    rank, features = adapter_down_weight.shape[1:]
    lane = lax.axis_index("tp")
    group = lax.axis_index("req")
    lane_arr = lane.reshape(1).astype(jnp.int32)

    down_row = lax.all_to_all(
        adapter_down_weight.reshape(LANES, rank // LANES, features), "tp", 0, 0, tiled=True
    )

    matches = block_adapter_ids[:, :, None] == jnp.arange(adapter_slot_table.shape[0], dtype=jnp.int32)
    slots = jnp.sum(jnp.where(matches, adapter_slot_table, 0), axis=2)
    here = slots // LANES == group
    wanted = jnp.sum(jnp.where(here, slots % LANES, 0), axis=1)
    wanted_shift = relative(lane, wanted)
    owner_rows = lax.dynamic_index_in_dim(slots, group, 0, keepdims=False) // LANES

    down_got = lax.all_to_all(pick_down(wanted, down_row), "req", 0, 0, tiled=True)

    up_pieces = split_up(lane_arr, adapter_up_weight)
    up_row = [up_pieces[0]] + [
        lax.ppermute(up_pieces[k], BOTH, lane_shift(groups, k // CORES, k % CORES)) for k in range(1, LANES)
    ]
    up_got = lax.all_to_all(pick_up(wanted_shift, up_row), "req", 0, 0, tiled=True)

    wide = hidden.astype(jnp.float32)
    inverse_rms = lax.rsqrt(jnp.mean(wide * wide, axis=-1, keepdims=True) + 1e-05)
    normed = (wide * inverse_rms * norm_gain_vector).astype(jnp.bfloat16)
    base = jnp.dot(normed, query_weight, preferred_element_type=jnp.float32)

    low = shrink(owner_rows, down_got, normed, blocks)
    other = lax.ppermute(low, BOTH, lane_shift(groups, 0, 1))
    chip = jnp.stack([low, other])
    lows = [chip] + [lax.ppermute(chip, BOTH, lane_shift(groups, dx, 0)) for dx in range(1, X)]
    return expand(owner_rows, lane_arr, base, lows, up_got, blocks)


def solution(mesh):
    return jax.shard_map(
        shards,
        mesh=mesh,
        in_specs=(
            P("req", None),
            P(),
            P(None, "tp"),
            P(("req", "tp"), None, None),
            P(("req", "tp"), None, None),
            P(),
            P(),
        ),
        out_specs=P("req", "tp"),
        check_vma=False,
    )
```

```python
import functools

import jax
import jax.numpy as jnp
from jax import lax
from jax.experimental import pallas as pl
from jax.experimental.pallas import tpu as pltpu
from jax.sharding import PartitionSpec as P

ADAPTER_SCALE = 0.5
X, CORES = 4, 2
LANES = X * CORES
BOTH = ("req", "tp")


def lane_shift(groups, dx, dc):
    return [
        (g * LANES + x * CORES + c, g * LANES + (x + dx) % X * CORES + (c + dc) % CORES)
        for g in range(groups)
        for x in range(X)
        for c in range(CORES)
    ]


def relative(lane, other):
    dx = (lane // CORES - other // CORES) % X
    dc = (lane % CORES - other % CORES) % CORES
    return dx * CORES + dc


def split_kernel(lane_ref, up_ref, *rest):
    outs, sems = rest[:LANES], rest[LANES]
    lane = lane_ref[0]
    width = outs[0].shape[1]
    copies = []
    for k in range(LANES):
        dx, dc = k // CORES, k % CORES
        to = (lane // CORES + dx) % X * CORES + (lane % CORES + dc) % CORES
        col = pl.multiple_of(to * width, width)
        copies.append(pltpu.make_async_copy(up_ref.at[0, :, pl.ds(col, width)], outs[k], sems.at[k]))
    for copy in copies:
        copy.start()
    for copy in copies:
        copy.wait()


def split_up(lane, up):
    rank, cols = up.shape[1:]
    width = cols // LANES
    any_spec = pl.BlockSpec(memory_space=pl.ANY)
    return pl.pallas_call(
        split_kernel,
        grid_spec=pltpu.PrefetchScalarGridSpec(
            num_scalar_prefetch=1,
            grid=(1,),
            in_specs=[pl.BlockSpec(up.shape, lambda i, lane: (0, 0, 0))],
            out_specs=[any_spec] * LANES,
            scratch_shapes=[pltpu.SemaphoreType.DMA((LANES,))],
        ),
        out_shape=[jax.ShapeDtypeStruct((rank, width), up.dtype)] * LANES,
        name="split_up",
    )(lane, up)


VMEM = pl.BlockSpec(memory_space=pltpu.VMEM)
SMEM = pl.BlockSpec(memory_space=pltpu.SMEM)


def pick_down_kernel(pick_ref, src_ref, out_ref):
    for g in range(out_ref.shape[0]):
        out_ref[g] = src_ref[pick_ref[g]]


def pick_down(pick, pieces):
    groups = pick.shape[0]
    return pl.pallas_call(
        pick_down_kernel,
        in_specs=[SMEM, VMEM],
        out_specs=VMEM,
        out_shape=jax.ShapeDtypeStruct((groups,) + pieces.shape[1:], pieces.dtype),
        compiler_params=pltpu.CompilerParams(vmem_limit_bytes=16 * 2**20),
        name="pick_down",
    )(pick, pieces)


def pick_up_kernel(pick_ref, *rest):
    srcs, out_ref = rest[:LANES], rest[LANES]
    for g in range(out_ref.shape[0]):
        for k in range(LANES):

            @pl.when(pick_ref[g] == k)
            def _():
                out_ref[g] = srcs[k][...]


def pick_up(pick, pieces):
    groups = pick.shape[0]
    return pl.pallas_call(
        pick_up_kernel,
        in_specs=[SMEM] + [VMEM] * LANES,
        out_specs=VMEM,
        out_shape=jax.ShapeDtypeStruct((groups,) + pieces[0].shape, pieces[0].dtype),
        compiler_params=pltpu.CompilerParams(vmem_limit_bytes=16 * 2**20),
        name="pick_up",
    )(pick, *pieces)


CHUNK = 1024
NORM_ROWS = 128


def norm_base_kernel(x_ref, gain_ref, weight_ref, *rest):
    normed_ref, base_ref = rest[-2:]
    rows, features = x_ref.shape
    squares = jnp.zeros((rows, 128), jnp.float32)
    for p in range(features // 128):
        wide = x_ref[:, p * 128 : (p + 1) * 128].astype(jnp.float32)
        squares = squares + wide * wide
    mean = jnp.sum(squares, axis=1, keepdims=True) / features
    inverse_rms = lax.rsqrt(mean + 1e-05)
    total = jnp.zeros(base_ref.shape, jnp.float32)
    for p in range(features // CHUNK):
        cols = slice(p * CHUNK, (p + 1) * CHUNK)
        wide = x_ref[:, cols].astype(jnp.float32)
        normed = (wide * inverse_rms * gain_ref[:, cols]).astype(jnp.bfloat16)
        normed_ref[:, cols] = normed
        total += jnp.dot(normed, weight_ref[cols, :], preferred_element_type=jnp.float32)
    base_ref[...] = total


def norm_base(hidden, gain, weight, first, last, done=None):
    rows, features = hidden.shape
    cols = weight.shape[1]
    count = last - first
    any_spec = pl.BlockSpec(memory_space=pl.ANY)
    return pl.pallas_call(
        norm_base_kernel,
        grid=(count,),
        in_specs=[
            pl.BlockSpec((NORM_ROWS, features), lambda i: (i + first, 0)),
            pl.BlockSpec((1, features), lambda i: (0, 0)),
            pl.BlockSpec((features, cols), lambda i: (0, 0), pipeline_mode=pl.Buffered(1)),
        ]
        + ([] if done is None else [any_spec, any_spec]),
        out_specs=[
            pl.BlockSpec((NORM_ROWS, features), lambda i: (i + first, 0)),
            pl.BlockSpec((NORM_ROWS, cols), lambda i: (i + first, 0)),
        ],
        out_shape=[
            jax.ShapeDtypeStruct((rows, features), jnp.bfloat16),
            jax.ShapeDtypeStruct((rows, cols), jnp.float32),
        ],
        input_output_aliases={} if done is None else {3: 0, 4: 1},
        compiler_params=pltpu.CompilerParams(vmem_limit_bytes=56 * 2**20),
        cost_estimate=pl.CostEstimate(
            flops=4 * NORM_ROWS * count * features * cols,
            bytes_accessed=4 * NORM_ROWS * count * features + 2 * features * cols,
            transcendentals=NORM_ROWS * count,
        ),
        name="norm_base",
    )(hidden, gain.reshape(1, features), weight, *(done or ()))


def shrink_kernel(row_ref, down_ref, normed_ref, low_ref):
    low_ref[0] = lax.dot_general(
        down_ref[0], normed_ref[...], (((1,), (1,)), ((), ())), preferred_element_type=jnp.float32
    )


def shrink(owner_rows, down_got, normed, blocks):
    rows, features = normed.shape
    block = rows // blocks
    part = down_got.shape[1]
    return pl.pallas_call(
        shrink_kernel,
        grid_spec=pltpu.PrefetchScalarGridSpec(
            num_scalar_prefetch=1,
            grid=(blocks,),
            in_specs=[
                pl.BlockSpec((1, part, features), lambda j, row: (row[j], 0, 0)),
                pl.BlockSpec((block, features), lambda j, row: (j, 0)),
            ],
            out_specs=pl.BlockSpec((1, part, block), lambda j, row: (j, 0, 0)),
        ),
        out_shape=jax.ShapeDtypeStruct((blocks, part, block), jnp.float32),
        compiler_params=pltpu.CompilerParams(vmem_limit_bytes=56 * 2**20),
        cost_estimate=pl.CostEstimate(
            flops=2 * rows * features * 256, bytes_accessed=2 * rows * features, transcendentals=0
        ),
        name="shrink",
    )(owner_rows, down_got, normed)


def expand_kernel(row_ref, lane_ref, base_ref, low0, low1, low2, low3, up_ref, out_ref, full):
    lows = (low0, low1, low2, low3)
    lane = lane_ref[0]
    blocks, part, block = low0.shape[1:]
    for dx in range(X):
        for dc in range(CORES):
            src = (lane // CORES - dx) % X * CORES + (lane % CORES - dc) % CORES
            rows = pl.ds(pl.multiple_of(src * part, part), part)
            for j in range(blocks):
                full[j, rows, :] = lows[dx][dc, j]
    for j in range(blocks):
        low = full[j].astype(jnp.bfloat16)
        term = lax.dot_general(
            low, up_ref[row_ref[j]], (((0,), (0,)), ((), ())), preferred_element_type=jnp.float32
        )
        rows = slice(j * block, (j + 1) * block)
        out_ref[rows, :] = (base_ref[rows, :] + ADAPTER_SCALE * term).astype(out_ref.dtype)


def expand(owner_rows, lane, base, lows, up_got, blocks):
    rows, cols = base.shape
    part = lows[0].shape[2]
    rank = up_got.shape[1]

    def whole(shape):
        return pl.BlockSpec(shape, lambda i, row, lane: (0,) * len(shape))

    return pl.pallas_call(
        expand_kernel,
        grid_spec=pltpu.PrefetchScalarGridSpec(
            num_scalar_prefetch=2,
            grid=(1,),
            in_specs=[whole(base.shape)] + [whole(low.shape) for low in lows] + [whole(up_got.shape)],
            out_specs=whole(base.shape),
            scratch_shapes=[pltpu.VMEM((blocks, rank, rows // blocks), jnp.float32)],
        ),
        out_shape=jax.ShapeDtypeStruct((rows, cols), jnp.bfloat16),
        compiler_params=pltpu.CompilerParams(vmem_limit_bytes=24 * 2**20),
        name="expand",
    )(owner_rows, lane, base, *lows, up_got)


def shards(
    hidden,
    norm_gain_vector,
    query_weight,
    adapter_down_weight,
    adapter_up_weight,
    block_adapter_ids,
    adapter_slot_table,
):
    groups, blocks = block_adapter_ids.shape
    rank, features = adapter_down_weight.shape[1:]
    lane = lax.axis_index("tp")
    group = lax.axis_index("req")
    lane_arr = lane.reshape(1).astype(jnp.int32)

    down_row = lax.all_to_all(
        adapter_down_weight.reshape(LANES, rank // LANES, features), "tp", 0, 0, tiled=True
    )

    matches = block_adapter_ids[:, :, None] == jnp.arange(adapter_slot_table.shape[0], dtype=jnp.int32)
    slots = jnp.sum(jnp.where(matches, adapter_slot_table, 0), axis=2)
    here = slots // LANES == group
    wanted = jnp.sum(jnp.where(here, slots % LANES, 0), axis=1)
    wanted_shift = relative(lane, wanted)
    owner_rows = lax.dynamic_index_in_dim(slots, group, 0, keepdims=False) // LANES

    up_pieces = split_up(lane_arr, adapter_up_weight)

    steps = hidden.shape[0] // NORM_ROWS
    cut = steps * 4 // 7
    done = norm_base(hidden, norm_gain_vector, query_weight, 0, cut)
    down_row, wanted, done, up_pieces = lax.optimization_barrier((down_row, wanted, done, up_pieces))

    down_send, done = lax.optimization_barrier((pick_down(wanted, down_row), done))
    down_got = lax.all_to_all(down_send, "req", 0, 0, tiled=True)

    up_row = [up_pieces[0]] + [
        lax.ppermute(up_pieces[k], BOTH, lane_shift(groups, k // CORES, k % CORES)) for k in range(1, LANES)
    ]
    normed, base = norm_base(hidden, norm_gain_vector, query_weight, cut, steps, done)
    down_got, up_send, normed, base = lax.optimization_barrier(
        (down_got, pick_up(wanted_shift, up_row), normed, base)
    )
    up_got = lax.all_to_all(up_send, "req", 0, 0, tiled=True)

    low = shrink(owner_rows, down_got, normed, blocks)
    other = lax.ppermute(low, BOTH, lane_shift(groups, 0, 1))
    chip = jnp.stack([low, other])
    lows = [chip] + [lax.ppermute(chip, BOTH, lane_shift(groups, dx, 0)) for dx in range(1, X)]
    return expand(owner_rows, lane_arr, base, lows, up_got, blocks)


def solution(mesh):
    return jax.shard_map(
        shards,
        mesh=mesh,
        in_specs=(
            P("req", None),
            P(),
            P(None, "tp"),
            P(("req", "tp"), None, None),
            P(("req", "tp"), None, None),
            P(),
            P(),
        ),
        out_specs=P("req", "tp"),
        check_vma=False,
    )
```

```python
import functools

import jax
import jax.numpy as jnp
from jax import lax
from jax.experimental import pallas as pl
from jax.experimental.pallas import tpu as pltpu
from jax.sharding import PartitionSpec as P

ADAPTER_SCALE = 0.5
X, CORES = 4, 2
LANES = X * CORES
ORDER = (2, 6, 3, 7, 4, 5, 1)
BOTH = ("req", "tp")


def lane_shift(groups, dx, dc):
    return [
        (g * LANES + x * CORES + c, g * LANES + (x + dx) % X * CORES + (c + dc) % CORES)
        for g in range(groups)
        for x in range(X)
        for c in range(CORES)
    ]


def relative(lane, other):
    dx = (lane // CORES - other // CORES) % X
    dc = (lane % CORES - other % CORES) % CORES
    return dx * CORES + dc


VMEM = pl.BlockSpec(memory_space=pltpu.VMEM)
SMEM = pl.BlockSpec(memory_space=pltpu.SMEM)
ANY = pl.BlockSpec(memory_space=pl.ANY)


def reached(lane, k):
    return (lane // CORES + k // CORES) % X * CORES + (lane % CORES + k % CORES) % CORES


def split_down_kernel(lane_ref, down_ref, *outs):
    for k in range(LANES):
        outs[k][...] = down_ref[reached(lane_ref[0], k)]


def split_up_kernel(lane_ref, up_ref, *outs):
    width = outs[0].shape[1]
    for k in range(LANES):
        col = pl.multiple_of(reached(lane_ref[0], k) * width, width)
        outs[k][...] = up_ref[0, :, pl.ds(col, width)]


def split(kernel, lane, whole, piece, name):
    return pl.pallas_call(
        kernel,
        in_specs=[SMEM, VMEM],
        out_specs=[VMEM] * LANES,
        out_shape=[jax.ShapeDtypeStruct(piece, whole.dtype)] * LANES,
        compiler_params=pltpu.CompilerParams(vmem_limit_bytes=16 * 2**20),
        name=name,
    )(lane, whole)


def spread(pieces, groups):
    return [
        lax.ppermute(pieces[k], BOTH, lane_shift(groups, k // CORES, k % CORES)) for k in ORDER
    ] + [pieces[0]]


def pick_kernel(pick_ref, *rest):
    srcs, out_ref, staged = rest[:LANES], rest[LANES], rest[LANES + 1]
    for src, k in zip(srcs, ORDER + (0,)):
        staged[k] = src[...]
    for g in range(out_ref.shape[0]):
        out_ref[g] = staged[pick_ref[g]]


def pick(shifts, pieces, name):
    groups = shifts.shape[0]
    shape, dtype = pieces[0].shape, pieces[0].dtype
    return pl.pallas_call(
        pick_kernel,
        in_specs=[SMEM] + [VMEM] * LANES,
        out_specs=VMEM,
        out_shape=jax.ShapeDtypeStruct((groups,) + shape, dtype),
        scratch_shapes=[pltpu.VMEM((LANES,) + shape, dtype)],
        compiler_params=pltpu.CompilerParams(vmem_limit_bytes=16 * 2**20),
        name=name,
    )(shifts, *pieces)


CHUNK = 1024
NORM_ROWS = 128


def norm_base_kernel(x_ref, gain_ref, weight_ref, normed_ref, base_ref):
    rows, features = x_ref.shape
    squares = jnp.zeros((rows, 128), jnp.float32)
    for p in range(features // 128):
        wide = x_ref[:, p * 128 : (p + 1) * 128].astype(jnp.float32)
        squares = squares + wide * wide
    mean = jnp.sum(squares, axis=1, keepdims=True) / features
    inverse_rms = lax.rsqrt(mean + 1e-05)
    total = jnp.zeros(base_ref.shape, jnp.float32)
    for p in range(features // CHUNK):
        cols = slice(p * CHUNK, (p + 1) * CHUNK)
        wide = x_ref[:, cols].astype(jnp.float32)
        normed = (wide * inverse_rms * gain_ref[:, cols]).astype(jnp.bfloat16)
        normed_ref[:, cols] = normed
        total += jnp.dot(normed, weight_ref[cols, :], preferred_element_type=jnp.float32)
    base_ref[...] = total


def norm_base(hidden, gain, weight):
    rows, features = hidden.shape
    cols = weight.shape[1]
    return pl.pallas_call(
        norm_base_kernel,
        grid=(rows // NORM_ROWS,),
        in_specs=[
            pl.BlockSpec((NORM_ROWS, features), lambda i: (i, 0)),
            pl.BlockSpec((1, features), lambda i: (0, 0)),
            pl.BlockSpec((features, cols), lambda i: (0, 0), pipeline_mode=pl.Buffered(1)),
        ],
        out_specs=[
            pl.BlockSpec((NORM_ROWS, features), lambda i: (i, 0)),
            pl.BlockSpec((NORM_ROWS, cols), lambda i: (i, 0)),
        ],
        out_shape=[
            jax.ShapeDtypeStruct((rows, features), jnp.bfloat16),
            jax.ShapeDtypeStruct((rows, cols), jnp.float32),
        ],
        compiler_params=pltpu.CompilerParams(vmem_limit_bytes=56 * 2**20),
        cost_estimate=pl.CostEstimate(
            flops=4 * rows * features * cols,
            bytes_accessed=4 * rows * features + 2 * features * cols,
            transcendentals=rows,
        ),
        name="norm_base",
    )(hidden, gain.reshape(1, features), weight)


def shrink_kernel(row_ref, down_ref, normed_hbm, low_ref, normed_ref, sems):
    blocks, block = low_ref.shape[0], low_ref.shape[2]

    def rows_of(j):
        return pl.ds(pl.multiple_of(j * block, block), block)

    def copy(j):
        return pltpu.make_async_copy(normed_hbm.at[rows_of(j)], normed_ref.at[rows_of(j)], sems.at[j])

    for j in range(blocks):
        copy(j).start()

    @pl.loop(0, blocks)
    def _(j):
        copy(j).wait()
        low_ref[j] = lax.dot_general(
            down_ref[row_ref[j]],
            normed_ref[rows_of(j), :],
            (((1,), (1,)), ((), ())),
            preferred_element_type=jnp.float32,
        )


def shrink(owner_rows, down_got, normed):
    blocks = owner_rows.shape[0]
    rows, features = normed.shape
    piece = down_got.shape[1]
    return pl.pallas_call(
        shrink_kernel,
        in_specs=[SMEM, VMEM, ANY],
        out_specs=VMEM,
        out_shape=jax.ShapeDtypeStruct((blocks, piece, rows // blocks), jnp.float32),
        scratch_shapes=[pltpu.VMEM((rows, features), jnp.bfloat16), pltpu.SemaphoreType.DMA((blocks,))],
        compiler_params=pltpu.CompilerParams(vmem_limit_bytes=48 * 2**20),
        cost_estimate=pl.CostEstimate(
            flops=2 * rows * features * 256, bytes_accessed=2 * rows * features, transcendentals=0
        ),
        name="shrink",
    )(owner_rows, down_got, normed)


def expand_kernel(row_ref, lane_ref, low0, low1, low2, low3, up_ref, base_ref, out_ref, full):
    lows = (low0, low1, low2, low3)
    lane = lane_ref[0]
    blocks, part, block = low0.shape[1:]
    for dx in range(X):
        for dc in range(CORES):
            src = (lane // CORES - dx) % X * CORES + (lane % CORES - dc) % CORES
            rows = pl.ds(pl.multiple_of(src * part, part), part)
            for j in range(blocks):
                full[j, rows, :] = lows[dx][dc, j]

    for j in range(blocks):
        low = full[j].astype(jnp.bfloat16)
        term = lax.dot_general(
            low, up_ref[row_ref[j]], (((0,), (0,)), ((), ())), preferred_element_type=jnp.float32
        )
        rows = slice(j * block, (j + 1) * block)
        out_ref[rows, :] = (base_ref[rows, :] + ADAPTER_SCALE * term).astype(out_ref.dtype)


def expand(owner_rows, lane, lows, up_got, base):
    blocks, part, block = lows[0].shape[1:]
    return pl.pallas_call(
        expand_kernel,
        in_specs=[SMEM, SMEM] + [VMEM] * (len(lows) + 2),
        out_specs=VMEM,
        out_shape=jax.ShapeDtypeStruct(base.shape, jnp.bfloat16),
        scratch_shapes=[pltpu.VMEM((blocks, part * LANES, block), jnp.float32)],
        compiler_params=pltpu.CompilerParams(vmem_limit_bytes=16 * 2**20),
        name="expand",
    )(owner_rows, lane, *lows, up_got, base)


def shards(
    hidden,
    norm_gain_vector,
    query_weight,
    adapter_down_weight,
    adapter_up_weight,
    block_adapter_ids,
    adapter_slot_table,
):
    groups, blocks = block_adapter_ids.shape
    rank, features = adapter_down_weight.shape[1:]
    lane = lax.axis_index("tp")
    group = lax.axis_index("req")
    lane_arr = lane.reshape(1).astype(jnp.int32)

    piece = (rank // LANES, features)
    down_whole = adapter_down_weight.reshape((LANES,) + piece)
    down_row = spread(split(split_down_kernel, lane_arr, down_whole, piece, "split_down"), groups)

    matches = block_adapter_ids[:, :, None] == jnp.arange(adapter_slot_table.shape[0], dtype=jnp.int32)
    slots = jnp.sum(jnp.where(matches, adapter_slot_table, 0), axis=2)
    here = slots // LANES == group
    wanted = relative(lane, jnp.sum(jnp.where(here, slots % LANES, 0), axis=1))
    owner_rows = lax.dynamic_index_in_dim(slots, group, 0, keepdims=False) // LANES

    down_send, hidden, adapter_up_weight = lax.optimization_barrier(
        (pick(wanted, down_row, "pick_down"), hidden, adapter_up_weight)
    )
    down_got = lax.all_to_all(down_send, "req", 0, 0, tiled=True)
    piece = (rank, adapter_up_weight.shape[2] // LANES)
    up_row = spread(split(split_up_kernel, lane_arr, adapter_up_weight, piece, "split_up"), groups)
    normed, base = norm_base(hidden, norm_gain_vector, query_weight)
    up_row, base = lax.optimization_barrier((up_row, base))
    up_got = lax.all_to_all(pick(wanted, up_row, "pick_up"), "req", 0, 0, tiled=True)

    low = shrink(owner_rows, down_got, normed)
    other = lax.ppermute(low, BOTH, lane_shift(groups, 0, 1))
    chip = jnp.stack([low, other])
    lows = [chip] + [lax.ppermute(chip, BOTH, lane_shift(groups, dx, 0)) for dx in range(1, X)]
    return expand(owner_rows, lane_arr, lows, up_got, base)


def solution(mesh):
    return jax.shard_map(
        shards,
        mesh=mesh,
        in_specs=(
            P("req", None),
            P(),
            P(None, "tp"),
            P(("req", "tp"), None, None),
            P(("req", "tp"), None, None),
            P(),
            P(),
        ),
        out_specs=P("req", "tp"),
        check_vma=False,
    )
```

```python
import functools

import jax
import jax.numpy as jnp
from jax import lax
from jax.experimental import pallas as pl
from jax.experimental.pallas import tpu as pltpu
from jax.sharding import PartitionSpec as P

ADAPTER_SCALE = 0.5
X, CORES = 4, 2
LANES = X * CORES
ORDER = (2, 6, 3, 7, 4, 5, 1)
BOTH = ("req", "tp")


def lane_shift(groups, dx, dc):
    return [
        (g * LANES + x * CORES + c, g * LANES + (x + dx) % X * CORES + (c + dc) % CORES)
        for g in range(groups)
        for x in range(X)
        for c in range(CORES)
    ]


def relative(lane, other):
    dx = (lane // CORES - other // CORES) % X
    dc = (lane % CORES - other % CORES) % CORES
    return dx * CORES + dc


VMEM = pl.BlockSpec(memory_space=pltpu.VMEM)
SMEM = pl.BlockSpec(memory_space=pltpu.SMEM)
ANY = pl.BlockSpec(memory_space=pl.ANY)


def reached(lane, k):
    return (lane // CORES + k // CORES) % X * CORES + (lane % CORES + k % CORES) % CORES


def split_down_kernel(lane_ref, down_ref, *outs):
    for k in range(LANES):
        outs[k][...] = down_ref[reached(lane_ref[0], k)]


def split_up_kernel(lane_ref, up_ref, *outs):
    width = outs[0].shape[1]
    for k in range(LANES):
        col = pl.multiple_of(reached(lane_ref[0], k) * width, width)
        outs[k][...] = up_ref[0, :, pl.ds(col, width)]


def split(kernel, lane, whole, piece, name):
    return pl.pallas_call(
        kernel,
        in_specs=[SMEM, VMEM],
        out_specs=[VMEM] * LANES,
        out_shape=[jax.ShapeDtypeStruct(piece, whole.dtype)] * LANES,
        compiler_params=pltpu.CompilerParams(vmem_limit_bytes=16 * 2**20),
        name=name,
    )(lane, whole)


def spread(pieces, groups):
    return [
        lax.ppermute(pieces[k], BOTH, lane_shift(groups, k // CORES, k % CORES)) for k in ORDER
    ] + [pieces[0]]


def pick_kernel(pick_ref, *rest):
    srcs, out_ref, staged = rest[:LANES], rest[LANES], rest[LANES + 1]
    for src, k in zip(srcs, ORDER + (0,)):
        staged[k] = src[...]
    for g in range(out_ref.shape[0]):
        out_ref[g] = staged[pick_ref[g]]


def pick(shifts, pieces, name):
    groups = shifts.shape[0]
    shape, dtype = pieces[0].shape, pieces[0].dtype
    return pl.pallas_call(
        pick_kernel,
        in_specs=[SMEM] + [VMEM] * LANES,
        out_specs=VMEM,
        out_shape=jax.ShapeDtypeStruct((groups,) + shape, dtype),
        scratch_shapes=[pltpu.VMEM((LANES,) + shape, dtype)],
        compiler_params=pltpu.CompilerParams(vmem_limit_bytes=16 * 2**20),
        name=name,
    )(shifts, *pieces)


CHUNK = 1024
NORM_ROWS = 128


def norm_base_kernel(x_ref, gain_ref, weight_ref, normed_ref, base_ref):
    rows, features = x_ref.shape
    squares = jnp.zeros((rows, 128), jnp.float32)
    for p in range(features // 128):
        wide = x_ref[:, p * 128 : (p + 1) * 128].astype(jnp.float32)
        squares = squares + wide * wide
    mean = jnp.sum(squares, axis=1, keepdims=True) / features
    inverse_rms = lax.rsqrt(mean + 1e-05)
    total = jnp.zeros(base_ref.shape, jnp.float32)
    for p in range(features // CHUNK):
        cols = slice(p * CHUNK, (p + 1) * CHUNK)
        wide = x_ref[:, cols].astype(jnp.float32)
        normed = (wide * inverse_rms * gain_ref[:, cols]).astype(jnp.bfloat16)
        normed_ref[:, cols] = normed
        total += jnp.dot(normed, weight_ref[cols, :], preferred_element_type=jnp.float32)
    base_ref[...] = total


def norm_base(hidden, gain, weight):
    rows, features = hidden.shape
    cols = weight.shape[1]
    return pl.pallas_call(
        norm_base_kernel,
        grid=(rows // NORM_ROWS,),
        in_specs=[
            pl.BlockSpec((NORM_ROWS, features), lambda i: (i, 0)),
            pl.BlockSpec((1, features), lambda i: (0, 0)),
            pl.BlockSpec((features, cols), lambda i: (0, 0), pipeline_mode=pl.Buffered(1)),
        ],
        out_specs=[
            pl.BlockSpec((NORM_ROWS, features), lambda i: (i, 0)),
            pl.BlockSpec((NORM_ROWS, cols), lambda i: (i, 0)),
        ],
        out_shape=[
            jax.ShapeDtypeStruct((rows, features), jnp.bfloat16),
            jax.ShapeDtypeStruct((rows, cols), jnp.float32),
        ],
        compiler_params=pltpu.CompilerParams(vmem_limit_bytes=56 * 2**20),
        cost_estimate=pl.CostEstimate(
            flops=4 * rows * features * cols,
            bytes_accessed=4 * rows * features + 2 * features * cols,
            transcendentals=rows,
        ),
        name="norm_base",
    )(hidden, gain.reshape(1, features), weight)


def shrink_kernel(row_ref, down_ref, normed_hbm, low_ref, normed_ref, sems):
    blocks, block = low_ref.shape[0], low_ref.shape[2]

    def rows_of(j):
        return pl.ds(pl.multiple_of(j * block, block), block)

    def copy(j):
        return pltpu.make_async_copy(normed_hbm.at[rows_of(j)], normed_ref.at[rows_of(j)], sems.at[j])

    for j in range(blocks):
        copy(j).start()

    @pl.loop(0, blocks)
    def _(j):
        copy(j).wait()
        low_ref[j] = lax.dot_general(
            down_ref[row_ref[j]],
            normed_ref[rows_of(j), :],
            (((1,), (1,)), ((), ())),
            preferred_element_type=jnp.float32,
        )


def shrink(owner_rows, down_got, normed):
    blocks = owner_rows.shape[0]
    rows, features = normed.shape
    piece = down_got.shape[1]
    return pl.pallas_call(
        shrink_kernel,
        in_specs=[SMEM, VMEM, ANY],
        out_specs=VMEM,
        out_shape=jax.ShapeDtypeStruct((blocks, piece, rows // blocks), jnp.float32),
        scratch_shapes=[pltpu.VMEM((rows, features), jnp.bfloat16), pltpu.SemaphoreType.DMA((blocks,))],
        compiler_params=pltpu.CompilerParams(vmem_limit_bytes=48 * 2**20),
        cost_estimate=pl.CostEstimate(
            flops=2 * rows * features * 256, bytes_accessed=2 * rows * features, transcendentals=0
        ),
        name="shrink",
    )(owner_rows, down_got, normed)


def gather_kernel(lane_ref, low0, low1, low2, low3, base_hbm, low_ref, base_ref, full, sem):
    copy = pltpu.make_async_copy(base_hbm, base_ref, sem)
    copy.start()
    lows = (low0, low1, low2, low3)
    lane = lane_ref[0]
    blocks, part, _ = low0.shape[1:]
    for dx in range(X):
        for dc in range(CORES):
            src = (lane // CORES - dx) % X * CORES + (lane % CORES - dc) % CORES
            rows = pl.ds(pl.multiple_of(src * part, part), part)
            for j in range(blocks):
                full[j, rows, :] = lows[dx][dc, j]
    for j in range(blocks):
        low_ref[j] = full[j].T.astype(low_ref.dtype)
    copy.wait()


def gather_low(lane, lows, base):
    blocks, part, block = lows[0].shape[1:]
    shape = (blocks, part * LANES, block)
    return pl.pallas_call(
        gather_kernel,
        in_specs=[SMEM] + [VMEM] * len(lows) + [ANY],
        out_specs=[VMEM, VMEM],
        out_shape=[
            jax.ShapeDtypeStruct((blocks, block, part * LANES), jnp.bfloat16),
            jax.ShapeDtypeStruct(base.shape, base.dtype),
        ],
        scratch_shapes=[pltpu.VMEM(shape, jnp.float32), pltpu.SemaphoreType.DMA],
        compiler_params=pltpu.CompilerParams(vmem_limit_bytes=16 * 2**20),
        name="gather_low",
    )(lane, *lows, base)


def expand_kernel(row_ref, low_ref, base_ref, up_ref, out_hbm, out_ref, sems):
    blocks, block, _ = low_ref.shape
    copies = []
    for j in range(blocks):
        rows = pl.ds(j * block, block)
        term = jnp.dot(low_ref[j], up_ref[row_ref[j]], preferred_element_type=jnp.float32)
        out_ref[rows, :] = (base_ref[rows, :] + ADAPTER_SCALE * term).astype(out_ref.dtype)
        copies.append(pltpu.make_async_copy(out_ref.at[rows], out_hbm.at[rows], sems.at[j]))
        copies[j].start()
    for copy in copies:
        copy.wait()


def expand(owner_rows, low, base, up_got):
    return pl.pallas_call(
        expand_kernel,
        in_specs=[SMEM, VMEM, VMEM, VMEM],
        out_specs=ANY,
        out_shape=jax.ShapeDtypeStruct(base.shape, jnp.bfloat16),
        scratch_shapes=[
            pltpu.VMEM(base.shape, jnp.bfloat16),
            pltpu.SemaphoreType.DMA((low.shape[0],)),
        ],
        compiler_params=pltpu.CompilerParams(vmem_limit_bytes=16 * 2**20),
        name="expand",
    )(owner_rows, low, base, up_got)


def shards(
    hidden,
    norm_gain_vector,
    query_weight,
    adapter_down_weight,
    adapter_up_weight,
    block_adapter_ids,
    adapter_slot_table,
):
    groups, blocks = block_adapter_ids.shape
    rank, features = adapter_down_weight.shape[1:]
    lane = lax.axis_index("tp")
    group = lax.axis_index("req")
    lane_arr = lane.reshape(1).astype(jnp.int32)

    piece = (rank // LANES, features)
    down_whole = adapter_down_weight.reshape((LANES,) + piece)
    down_row = spread(split(split_down_kernel, lane_arr, down_whole, piece, "split_down"), groups)

    matches = block_adapter_ids[:, :, None] == jnp.arange(adapter_slot_table.shape[0], dtype=jnp.int32)
    slots = jnp.sum(jnp.where(matches, adapter_slot_table, 0), axis=2)
    here = slots // LANES == group
    wanted = relative(lane, jnp.sum(jnp.where(here, slots % LANES, 0), axis=1))
    owner_rows = lax.dynamic_index_in_dim(slots, group, 0, keepdims=False) // LANES

    down_send, hidden, adapter_up_weight = lax.optimization_barrier(
        (pick(wanted, down_row, "pick_down"), hidden, adapter_up_weight)
    )
    down_got = lax.all_to_all(down_send, "req", 0, 0, tiled=True)
    piece = (rank, adapter_up_weight.shape[2] // LANES)
    up_row = spread(split(split_up_kernel, lane_arr, adapter_up_weight, piece, "split_up"), groups)
    normed, base = norm_base(hidden, norm_gain_vector, query_weight)
    up_row, base = lax.optimization_barrier((up_row, base))
    up_got = lax.all_to_all(pick(wanted, up_row, "pick_up"), "req", 0, 0, tiled=True)

    low = shrink(owner_rows, down_got, normed)
    other = lax.ppermute(low, BOTH, lane_shift(groups, 0, 1))
    chip = jnp.stack([low, other])
    lows = [chip] + [lax.ppermute(chip, BOTH, lane_shift(groups, dx, 0)) for dx in range(1, X)]
    low, base = gather_low(lane_arr, lows, base)
    return expand(owner_rows, low, base, up_got)


def solution(mesh):
    return jax.shard_map(
        shards,
        mesh=mesh,
        in_specs=(
            P("req", None),
            P(),
            P(None, "tp"),
            P(("req", "tp"), None, None),
            P(("req", "tp"), None, None),
            P(),
            P(),
        ),
        out_specs=P("req", "tp"),
        check_vma=False,
    )
```

```python
import functools

import jax
import jax.numpy as jnp
from jax import lax
from jax.experimental import pallas as pl
from jax.experimental.pallas import tpu as pltpu
from jax.sharding import PartitionSpec as P

ADAPTER_SCALE = 0.5
X, CORES = 4, 2
LANES = X * CORES
ORDER = (2, 6, 3, 7, 4, 5, 1)
BOTH = ("req", "tp")


def lane_shift(groups, dx, dc):
    return [
        (g * LANES + x * CORES + c, g * LANES + (x + dx) % X * CORES + (c + dc) % CORES)
        for g in range(groups)
        for x in range(X)
        for c in range(CORES)
    ]


def relative(lane, other):
    dx = (lane // CORES - other // CORES) % X
    dc = (lane % CORES - other % CORES) % CORES
    return dx * CORES + dc


VMEM = pl.BlockSpec(memory_space=pltpu.VMEM)
SMEM = pl.BlockSpec(memory_space=pltpu.SMEM)
ANY = pl.BlockSpec(memory_space=pl.ANY)


def reached(lane, k):
    return (lane // CORES + k // CORES) % X * CORES + (lane % CORES + k % CORES) % CORES


def split_down_kernel(lane_ref, down_ref, *outs):
    for k in range(LANES):
        outs[k][...] = down_ref[reached(lane_ref[0], k)]


def split_up_kernel(lane_ref, up_ref, same_ref, cross_ref):
    width = same_ref.shape[2]
    for dx in range(X):
        for dc, out_ref in enumerate((same_ref, cross_ref)):
            col = pl.multiple_of(reached(lane_ref[0], dx * CORES + dc) * width, width)
            out_ref[dx] = up_ref[0, :, pl.ds(col, width)]


def split_up(lane, up):
    rank, cols = up.shape[1:]
    return pl.pallas_call(
        split_up_kernel,
        in_specs=[SMEM, VMEM],
        out_specs=[VMEM, VMEM],
        out_shape=[jax.ShapeDtypeStruct((X, rank, cols // LANES), up.dtype)] * CORES,
        compiler_params=pltpu.CompilerParams(vmem_limit_bytes=16 * 2**20),
        name="split_up",
    )(lane, up)


def pair_kernel(same_ref, cross_ref, *outs):
    for dx in range(X):
        outs[dx][0] = same_ref[dx]
        outs[dx][1] = cross_ref[dx]


def pair_up(same, cross):
    shape = (CORES,) + same.shape[1:]
    return pl.pallas_call(
        pair_kernel,
        in_specs=[VMEM, VMEM],
        out_specs=[VMEM] * X,
        out_shape=[jax.ShapeDtypeStruct(shape, same.dtype)] * X,
        compiler_params=pltpu.CompilerParams(vmem_limit_bytes=16 * 2**20),
        name="pair_up",
    )(same, cross)


def pick_up_kernel(pick_ref, *rest):
    srcs, out_ref, staged = rest[:X], rest[X], rest[X + 1]
    for dx in range(X):
        for dc in range(CORES):
            staged[dx * CORES + dc] = srcs[dx][dc]
    for g in range(out_ref.shape[0]):
        out_ref[g] = staged[pick_ref[g]]


def pick_up(shifts, pairs):
    groups = shifts.shape[0]
    shape, dtype = pairs[0].shape[1:], pairs[0].dtype
    return pl.pallas_call(
        pick_up_kernel,
        in_specs=[SMEM] + [VMEM] * X,
        out_specs=VMEM,
        out_shape=jax.ShapeDtypeStruct((groups,) + shape, dtype),
        scratch_shapes=[pltpu.VMEM((LANES,) + shape, dtype)],
        compiler_params=pltpu.CompilerParams(vmem_limit_bytes=16 * 2**20),
        name="pick_up",
    )(shifts, *pairs)


def split(kernel, lane, whole, piece, name):
    return pl.pallas_call(
        kernel,
        in_specs=[SMEM, VMEM],
        out_specs=[VMEM] * LANES,
        out_shape=[jax.ShapeDtypeStruct(piece, whole.dtype)] * LANES,
        compiler_params=pltpu.CompilerParams(vmem_limit_bytes=16 * 2**20),
        name=name,
    )(lane, whole)


def spread(pieces, groups):
    return [
        lax.ppermute(pieces[k], BOTH, lane_shift(groups, k // CORES, k % CORES)) for k in ORDER
    ] + [pieces[0]]


def pick_kernel(pick_ref, *rest):
    srcs, out_ref, staged = rest[:LANES], rest[LANES], rest[LANES + 1]
    for src, k in zip(srcs, ORDER + (0,)):
        staged[k] = src[...]
    for g in range(out_ref.shape[0]):
        out_ref[g] = staged[pick_ref[g]]


def pick(shifts, pieces, name):
    groups = shifts.shape[0]
    shape, dtype = pieces[0].shape, pieces[0].dtype
    return pl.pallas_call(
        pick_kernel,
        in_specs=[SMEM] + [VMEM] * LANES,
        out_specs=VMEM,
        out_shape=jax.ShapeDtypeStruct((groups,) + shape, dtype),
        scratch_shapes=[pltpu.VMEM((LANES,) + shape, dtype)],
        compiler_params=pltpu.CompilerParams(vmem_limit_bytes=16 * 2**20),
        name=name,
    )(shifts, *pieces)


CHUNK = 1024
NORM_ROWS = 128


def norm_base_kernel(x_ref, gain_ref, weight_ref, normed_ref, base_ref):
    rows, features = x_ref.shape
    squares = jnp.zeros((rows, 128), jnp.float32)
    for p in range(features // 128):
        wide = x_ref[:, p * 128 : (p + 1) * 128].astype(jnp.float32)
        squares = squares + wide * wide
    mean = jnp.sum(squares, axis=1, keepdims=True) / features
    inverse_rms = lax.rsqrt(mean + 1e-05)
    total = jnp.zeros(base_ref.shape, jnp.float32)
    for p in range(features // CHUNK):
        cols = slice(p * CHUNK, (p + 1) * CHUNK)
        wide = x_ref[:, cols].astype(jnp.float32)
        normed = (wide * inverse_rms * gain_ref[:, cols]).astype(jnp.bfloat16)
        normed_ref[:, cols] = normed
        total += jnp.dot(normed, weight_ref[cols, :], preferred_element_type=jnp.float32)
    base_ref[...] = total


def norm_base(hidden, gain, weight):
    rows, features = hidden.shape
    cols = weight.shape[1]
    return pl.pallas_call(
        norm_base_kernel,
        grid=(rows // NORM_ROWS,),
        in_specs=[
            pl.BlockSpec((NORM_ROWS, features), lambda i: (i, 0)),
            pl.BlockSpec((1, features), lambda i: (0, 0)),
            pl.BlockSpec((features, cols), lambda i: (0, 0), pipeline_mode=pl.Buffered(1)),
        ],
        out_specs=[
            pl.BlockSpec((NORM_ROWS, features), lambda i: (i, 0)),
            pl.BlockSpec((NORM_ROWS, cols), lambda i: (i, 0)),
        ],
        out_shape=[
            jax.ShapeDtypeStruct((rows, features), jnp.bfloat16),
            jax.ShapeDtypeStruct((rows, cols), jnp.float32),
        ],
        compiler_params=pltpu.CompilerParams(vmem_limit_bytes=56 * 2**20),
        cost_estimate=pl.CostEstimate(
            flops=4 * rows * features * cols,
            bytes_accessed=4 * rows * features + 2 * features * cols,
            transcendentals=rows,
        ),
        name="norm_base",
    )(hidden, gain.reshape(1, features), weight)


def shrink_kernel(row_ref, down_ref, normed_hbm, low_ref, normed_ref, sems):
    blocks, block = low_ref.shape[0], low_ref.shape[2]

    def rows_of(j):
        return pl.ds(pl.multiple_of(j * block, block), block)

    def copy(j):
        return pltpu.make_async_copy(normed_hbm.at[rows_of(j)], normed_ref.at[rows_of(j)], sems.at[j])

    for j in range(blocks):
        copy(j).start()

    @pl.loop(0, blocks)
    def _(j):
        copy(j).wait()
        low_ref[j] = lax.dot_general(
            down_ref[row_ref[j]],
            normed_ref[rows_of(j), :],
            (((1,), (1,)), ((), ())),
            preferred_element_type=jnp.float32,
        )


def shrink(owner_rows, down_got, normed):
    blocks = owner_rows.shape[0]
    rows, features = normed.shape
    piece = down_got.shape[1]
    return pl.pallas_call(
        shrink_kernel,
        in_specs=[SMEM, VMEM, ANY],
        out_specs=VMEM,
        out_shape=jax.ShapeDtypeStruct((blocks, piece, rows // blocks), jnp.float32),
        scratch_shapes=[pltpu.VMEM((rows, features), jnp.bfloat16), pltpu.SemaphoreType.DMA((blocks,))],
        compiler_params=pltpu.CompilerParams(vmem_limit_bytes=48 * 2**20),
        cost_estimate=pl.CostEstimate(
            flops=2 * rows * features * 256, bytes_accessed=2 * rows * features, transcendentals=0
        ),
        name="shrink",
    )(owner_rows, down_got, normed)


def gather_kernel(lane_ref, low0, low1, low2, low3, base_hbm, low_ref, base_ref, full, sem):
    copy = pltpu.make_async_copy(base_hbm, base_ref, sem)
    copy.start()
    lows = (low0, low1, low2, low3)
    lane = lane_ref[0]
    blocks, part, _ = low0.shape[1:]
    for dx in range(X):
        for dc in range(CORES):
            src = (lane // CORES - dx) % X * CORES + (lane % CORES - dc) % CORES
            rows = pl.ds(pl.multiple_of(src * part, part), part)
            for j in range(blocks):
                full[j, rows, :] = lows[dx][dc, j]
    for j in range(blocks):
        low_ref[j] = full[j].T.astype(low_ref.dtype)
    copy.wait()


def gather_low(lane, lows, base):
    blocks, part, block = lows[0].shape[1:]
    shape = (blocks, part * LANES, block)
    return pl.pallas_call(
        gather_kernel,
        in_specs=[SMEM] + [VMEM] * len(lows) + [ANY],
        out_specs=[VMEM, VMEM],
        out_shape=[
            jax.ShapeDtypeStruct((blocks, block, part * LANES), jnp.bfloat16),
            jax.ShapeDtypeStruct(base.shape, base.dtype),
        ],
        scratch_shapes=[pltpu.VMEM(shape, jnp.float32), pltpu.SemaphoreType.DMA],
        compiler_params=pltpu.CompilerParams(vmem_limit_bytes=16 * 2**20),
        name="gather_low",
    )(lane, *lows, base)


def expand_kernel(row_ref, low_ref, base_ref, up_ref, out_hbm, out_ref, sems):
    blocks, block, _ = low_ref.shape
    copies = []
    for j in range(blocks):
        rows = pl.ds(j * block, block)
        term = jnp.dot(low_ref[j], up_ref[row_ref[j]], preferred_element_type=jnp.float32)
        out_ref[rows, :] = (base_ref[rows, :] + ADAPTER_SCALE * term).astype(out_ref.dtype)
        copies.append(pltpu.make_async_copy(out_ref.at[rows], out_hbm.at[rows], sems.at[j]))
        copies[j].start()
    for copy in copies:
        copy.wait()


def expand(owner_rows, low, base, up_got):
    return pl.pallas_call(
        expand_kernel,
        in_specs=[SMEM, VMEM, VMEM, VMEM],
        out_specs=ANY,
        out_shape=jax.ShapeDtypeStruct(base.shape, jnp.bfloat16),
        scratch_shapes=[
            pltpu.VMEM(base.shape, jnp.bfloat16),
            pltpu.SemaphoreType.DMA((low.shape[0],)),
        ],
        compiler_params=pltpu.CompilerParams(vmem_limit_bytes=16 * 2**20),
        name="expand",
    )(owner_rows, low, base, up_got)


def shards(
    hidden,
    norm_gain_vector,
    query_weight,
    adapter_down_weight,
    adapter_up_weight,
    block_adapter_ids,
    adapter_slot_table,
):
    groups, blocks = block_adapter_ids.shape
    rank, features = adapter_down_weight.shape[1:]
    lane = lax.axis_index("tp")
    group = lax.axis_index("req")
    lane_arr = lane.reshape(1).astype(jnp.int32)

    piece = (rank // LANES, features)
    down_whole = adapter_down_weight.reshape((LANES,) + piece)
    down_row = spread(split(split_down_kernel, lane_arr, down_whole, piece, "split_down"), groups)

    matches = block_adapter_ids[:, :, None] == jnp.arange(adapter_slot_table.shape[0], dtype=jnp.int32)
    slots = jnp.sum(jnp.where(matches, adapter_slot_table, 0), axis=2)
    here = slots // LANES == group
    wanted = relative(lane, jnp.sum(jnp.where(here, slots % LANES, 0), axis=1))
    owner_rows = lax.dynamic_index_in_dim(slots, group, 0, keepdims=False) // LANES

    down_send, hidden, adapter_up_weight = lax.optimization_barrier(
        (pick(wanted, down_row, "pick_down"), hidden, adapter_up_weight)
    )
    down_got = lax.all_to_all(down_send, "req", 0, 0, tiled=True)
    same, cross = split_up(lane_arr, adapter_up_weight)
    cross = lax.ppermute(cross, BOTH, lane_shift(groups, 0, 1))
    pairs = pair_up(same, cross)
    pairs = [pairs[0]] + [lax.ppermute(pairs[dx], BOTH, lane_shift(groups, dx, 0)) for dx in range(1, X)]
    normed, base = norm_base(hidden, norm_gain_vector, query_weight)
    pairs, base = lax.optimization_barrier((pairs, base))
    up_got = lax.all_to_all(pick_up(wanted, pairs), "req", 0, 0, tiled=True)

    low = shrink(owner_rows, down_got, normed)
    other = lax.ppermute(low, BOTH, lane_shift(groups, 0, 1))
    chip = jnp.stack([low, other])
    lows = [chip] + [lax.ppermute(chip, BOTH, lane_shift(groups, dx, 0)) for dx in range(1, X)]
    low, base = gather_low(lane_arr, lows, base)
    return expand(owner_rows, low, base, up_got)


def solution(mesh):
    return jax.shard_map(
        shards,
        mesh=mesh,
        in_specs=(
            P("req", None),
            P(),
            P(None, "tp"),
            P(("req", "tp"), None, None),
            P(("req", "tp"), None, None),
            P(),
            P(),
        ),
        out_specs=P("req", "tp"),
        check_vma=False,
    )
```

```python
import functools

import jax
import jax.numpy as jnp
from jax import lax
from jax.experimental import pallas as pl
from jax.experimental.pallas import tpu as pltpu
from jax.sharding import PartitionSpec as P

ADAPTER_SCALE = 0.5
X, CORES = 4, 2
LANES = X * CORES
ORDER = (4, 5, 2, 6, 3, 7, 1)
BOTH = ("req", "tp")


def lane_shift(groups, dx, dc):
    return [
        (g * LANES + x * CORES + c, g * LANES + (x + dx) % X * CORES + (c + dc) % CORES)
        for g in range(groups)
        for x in range(X)
        for c in range(CORES)
    ]


def relative(lane, other):
    dx = (lane // CORES - other // CORES) % X
    dc = (lane % CORES - other % CORES) % CORES
    return dx * CORES + dc


VMEM = pl.BlockSpec(memory_space=pltpu.VMEM)
SMEM = pl.BlockSpec(memory_space=pltpu.SMEM)
ANY = pl.BlockSpec(memory_space=pl.ANY)


def reached(lane, k):
    return (lane // CORES + k // CORES) % X * CORES + (lane % CORES + k % CORES) % CORES


def split_down_kernel(lane_ref, down_ref, *outs):
    for k in range(LANES):
        outs[k][...] = down_ref[reached(lane_ref[0], k)]


def split_up_kernel(lane_ref, up_ref, same_ref, cross_ref):
    width = same_ref.shape[2]
    for dx in range(X):
        for dc, out_ref in enumerate((same_ref, cross_ref)):
            col = pl.multiple_of(reached(lane_ref[0], dx * CORES + dc) * width, width)
            out_ref[dx] = up_ref[0, :, pl.ds(col, width)]


def split_up(lane, up):
    rank, cols = up.shape[1:]
    return pl.pallas_call(
        split_up_kernel,
        in_specs=[SMEM, VMEM],
        out_specs=[VMEM, VMEM],
        out_shape=[jax.ShapeDtypeStruct((X, rank, cols // LANES), up.dtype)] * CORES,
        compiler_params=pltpu.CompilerParams(vmem_limit_bytes=16 * 2**20),
        name="split_up",
    )(lane, up)


def pair_kernel(same_ref, cross_ref, *outs):
    for dx in range(X):
        outs[dx][0] = same_ref[dx]
        outs[dx][1] = cross_ref[dx]


def pair_up(same, cross):
    shape = (CORES,) + same.shape[1:]
    return pl.pallas_call(
        pair_kernel,
        in_specs=[VMEM, VMEM],
        out_specs=[VMEM] * X,
        out_shape=[jax.ShapeDtypeStruct(shape, same.dtype)] * X,
        compiler_params=pltpu.CompilerParams(vmem_limit_bytes=16 * 2**20),
        name="pair_up",
    )(same, cross)


def pick_up_kernel(pick_ref, *rest):
    srcs, out_ref, staged = rest[:X], rest[X], rest[X + 1]
    for dx in range(X):
        for dc in range(CORES):
            staged[dx * CORES + dc] = srcs[dx][dc]
    for g in range(out_ref.shape[0]):
        out_ref[g] = staged[pick_ref[g]]


def pick_up(shifts, pairs):
    groups = shifts.shape[0]
    shape, dtype = pairs[0].shape[1:], pairs[0].dtype
    return pl.pallas_call(
        pick_up_kernel,
        in_specs=[SMEM] + [VMEM] * X,
        out_specs=VMEM,
        out_shape=jax.ShapeDtypeStruct((groups,) + shape, dtype),
        scratch_shapes=[pltpu.VMEM((LANES,) + shape, dtype)],
        compiler_params=pltpu.CompilerParams(vmem_limit_bytes=16 * 2**20),
        name="pick_up",
    )(shifts, *pairs)


def split(kernel, lane, whole, piece, name):
    return pl.pallas_call(
        kernel,
        in_specs=[SMEM, VMEM],
        out_specs=[VMEM] * LANES,
        out_shape=[jax.ShapeDtypeStruct(piece, whole.dtype)] * LANES,
        compiler_params=pltpu.CompilerParams(vmem_limit_bytes=16 * 2**20),
        name=name,
    )(lane, whole)


def spread(pieces, groups):
    return [
        lax.ppermute(pieces[k], BOTH, lane_shift(groups, k // CORES, k % CORES)) for k in ORDER
    ] + [pieces[0]]


def pick_kernel(pick_ref, *rest):
    srcs, out_ref, staged = rest[:LANES], rest[LANES], rest[LANES + 1]
    for src, k in zip(srcs, ORDER + (0,)):
        staged[k] = src[...]
    for g in range(out_ref.shape[0]):
        out_ref[g] = staged[pick_ref[g]]


def pick(shifts, pieces, name):
    groups = shifts.shape[0]
    shape, dtype = pieces[0].shape, pieces[0].dtype
    return pl.pallas_call(
        pick_kernel,
        in_specs=[SMEM] + [VMEM] * LANES,
        out_specs=VMEM,
        out_shape=jax.ShapeDtypeStruct((groups,) + shape, dtype),
        scratch_shapes=[pltpu.VMEM((LANES,) + shape, dtype)],
        compiler_params=pltpu.CompilerParams(vmem_limit_bytes=16 * 2**20),
        name=name,
    )(shifts, *pieces)


CHUNK = 1024
NORM_ROWS = 128


def norm_base_kernel(x_ref, gain_ref, weight_ref, normed_ref, base_ref):
    rows, features = x_ref.shape
    squares = jnp.zeros((rows, 128), jnp.float32)
    for p in range(features // 128):
        wide = x_ref[:, p * 128 : (p + 1) * 128].astype(jnp.float32)
        squares = squares + wide * wide
    mean = jnp.sum(squares, axis=1, keepdims=True) / features
    inverse_rms = lax.rsqrt(mean + 1e-05)
    total = jnp.zeros(base_ref.shape, jnp.float32)
    for p in range(features // CHUNK):
        cols = slice(p * CHUNK, (p + 1) * CHUNK)
        wide = x_ref[:, cols].astype(jnp.float32)
        normed = (wide * inverse_rms * gain_ref[:, cols]).astype(jnp.bfloat16)
        normed_ref[:, cols] = normed
        total += jnp.dot(normed, weight_ref[cols, :], preferred_element_type=jnp.float32)
    base_ref[...] = total


def norm_base(hidden, gain, weight):
    rows, features = hidden.shape
    cols = weight.shape[1]
    return pl.pallas_call(
        norm_base_kernel,
        grid=(rows // NORM_ROWS,),
        in_specs=[
            pl.BlockSpec((NORM_ROWS, features), lambda i: (i, 0)),
            pl.BlockSpec((1, features), lambda i: (0, 0)),
            pl.BlockSpec((features, cols), lambda i: (0, 0), pipeline_mode=pl.Buffered(1)),
        ],
        out_specs=[
            pl.BlockSpec((NORM_ROWS, features), lambda i: (i, 0)),
            pl.BlockSpec((NORM_ROWS, cols), lambda i: (i, 0)),
        ],
        out_shape=[
            jax.ShapeDtypeStruct((rows, features), jnp.bfloat16),
            jax.ShapeDtypeStruct((rows, cols), jnp.float32),
        ],
        compiler_params=pltpu.CompilerParams(vmem_limit_bytes=56 * 2**20),
        cost_estimate=pl.CostEstimate(
            flops=4 * rows * features * cols,
            bytes_accessed=4 * rows * features + 2 * features * cols,
            transcendentals=rows,
        ),
        name="norm_base",
    )(hidden, gain.reshape(1, features), weight)


def shrink_kernel(row_ref, down_ref, normed_hbm, low_ref, normed_ref, sems):
    blocks, block = low_ref.shape[0], low_ref.shape[2]

    def rows_of(j):
        return pl.ds(pl.multiple_of(j * block, block), block)

    def copy(j):
        return pltpu.make_async_copy(normed_hbm.at[rows_of(j)], normed_ref.at[rows_of(j)], sems.at[j])

    for j in range(blocks):
        copy(j).start()

    @pl.loop(0, blocks)
    def _(j):
        copy(j).wait()
        low_ref[j] = lax.dot_general(
            down_ref[row_ref[j]],
            normed_ref[rows_of(j), :],
            (((1,), (1,)), ((), ())),
            preferred_element_type=jnp.float32,
        )


def shrink(owner_rows, down_got, normed):
    blocks = owner_rows.shape[0]
    rows, features = normed.shape
    piece = down_got.shape[1]
    return pl.pallas_call(
        shrink_kernel,
        in_specs=[SMEM, VMEM, ANY],
        out_specs=VMEM,
        out_shape=jax.ShapeDtypeStruct((blocks, piece, rows // blocks), jnp.float32),
        scratch_shapes=[pltpu.VMEM((rows, features), jnp.bfloat16), pltpu.SemaphoreType.DMA((blocks,))],
        compiler_params=pltpu.CompilerParams(vmem_limit_bytes=48 * 2**20),
        cost_estimate=pl.CostEstimate(
            flops=2 * rows * features * 256, bytes_accessed=2 * rows * features, transcendentals=0
        ),
        name="shrink",
    )(owner_rows, down_got, normed)


def gather_kernel(lane_ref, low0, low1, low2, low3, base_hbm, low_ref, base_ref, full, sem):
    copy = pltpu.make_async_copy(base_hbm, base_ref, sem)
    copy.start()
    lows = (low0, low1, low2, low3)
    lane = lane_ref[0]
    blocks, part, _ = low0.shape[1:]
    for dx in range(X):
        for dc in range(CORES):
            src = (lane // CORES - dx) % X * CORES + (lane % CORES - dc) % CORES
            rows = pl.ds(pl.multiple_of(src * part, part), part)
            for j in range(blocks):
                full[j, rows, :] = lows[dx][dc, j]
    for j in range(blocks):
        low_ref[j] = full[j].T.astype(low_ref.dtype)
    copy.wait()


def gather_low(lane, lows, base):
    blocks, part, block = lows[0].shape[1:]
    shape = (blocks, part * LANES, block)
    return pl.pallas_call(
        gather_kernel,
        in_specs=[SMEM] + [VMEM] * len(lows) + [ANY],
        out_specs=[VMEM, VMEM],
        out_shape=[
            jax.ShapeDtypeStruct((blocks, block, part * LANES), jnp.bfloat16),
            jax.ShapeDtypeStruct(base.shape, base.dtype),
        ],
        scratch_shapes=[pltpu.VMEM(shape, jnp.float32), pltpu.SemaphoreType.DMA],
        compiler_params=pltpu.CompilerParams(vmem_limit_bytes=16 * 2**20),
        name="gather_low",
    )(lane, *lows, base)


def expand_kernel(row_ref, low_ref, base_ref, up_ref, out_hbm, out_ref, sems):
    blocks, block, _ = low_ref.shape
    copies = []
    for j in range(blocks):
        rows = pl.ds(j * block, block)
        term = jnp.dot(low_ref[j], up_ref[row_ref[j]], preferred_element_type=jnp.float32)
        out_ref[rows, :] = (base_ref[rows, :] + ADAPTER_SCALE * term).astype(out_ref.dtype)
        copies.append(pltpu.make_async_copy(out_ref.at[rows], out_hbm.at[rows], sems.at[j]))
        copies[j].start()
    for copy in copies:
        copy.wait()


def expand(owner_rows, low, base, up_got):
    return pl.pallas_call(
        expand_kernel,
        in_specs=[SMEM, VMEM, VMEM, VMEM],
        out_specs=ANY,
        out_shape=jax.ShapeDtypeStruct(base.shape, jnp.bfloat16),
        scratch_shapes=[
            pltpu.VMEM(base.shape, jnp.bfloat16),
            pltpu.SemaphoreType.DMA((low.shape[0],)),
        ],
        compiler_params=pltpu.CompilerParams(vmem_limit_bytes=16 * 2**20),
        name="expand",
    )(owner_rows, low, base, up_got)


def shards(
    hidden,
    norm_gain_vector,
    query_weight,
    adapter_down_weight,
    adapter_up_weight,
    block_adapter_ids,
    adapter_slot_table,
):
    groups, blocks = block_adapter_ids.shape
    rank, features = adapter_down_weight.shape[1:]
    lane = lax.axis_index("tp")
    group = lax.axis_index("req")
    lane_arr = lane.reshape(1).astype(jnp.int32)

    piece = (rank // LANES, features)
    down_whole = adapter_down_weight.reshape((LANES,) + piece)
    down_row = spread(split(split_down_kernel, lane_arr, down_whole, piece, "split_down"), groups)

    matches = block_adapter_ids[:, :, None] == jnp.arange(adapter_slot_table.shape[0], dtype=jnp.int32)
    slots = jnp.sum(jnp.where(matches, adapter_slot_table, 0), axis=2)
    here = slots // LANES == group
    wanted = relative(lane, jnp.sum(jnp.where(here, slots % LANES, 0), axis=1))
    owner_rows = lax.dynamic_index_in_dim(slots, group, 0, keepdims=False) // LANES

    down_send, hidden, adapter_up_weight = lax.optimization_barrier(
        (pick(wanted, down_row, "pick_down"), hidden, adapter_up_weight)
    )
    down_got = lax.all_to_all(down_send, "req", 0, 0, tiled=True)
    same, cross = split_up(lane_arr, adapter_up_weight)
    cross = lax.ppermute(cross, BOTH, lane_shift(groups, 0, 1))
    pairs = pair_up(same, cross)
    pairs = [pairs[0]] + [lax.ppermute(pairs[dx], BOTH, lane_shift(groups, dx, 0)) for dx in range(1, X)]
    normed, base = norm_base(hidden, norm_gain_vector, query_weight)
    pairs, base = lax.optimization_barrier((pairs, base))
    up_got = lax.all_to_all(pick_up(wanted, pairs), "req", 0, 0, tiled=True)

    low = shrink(owner_rows, down_got, normed)
    other = lax.ppermute(low, BOTH, lane_shift(groups, 0, 1))
    chip = jnp.stack([low, other])
    lows = [chip] + [lax.ppermute(chip, BOTH, lane_shift(groups, dx, 0)) for dx in range(1, X)]
    low, base = gather_low(lane_arr, lows, base)
    return expand(owner_rows, low, base, up_got)


def solution(mesh):
    return jax.shard_map(
        shards,
        mesh=mesh,
        in_specs=(
            P("req", None),
            P(),
            P(None, "tp"),
            P(("req", "tp"), None, None),
            P(("req", "tp"), None, None),
            P(),
            P(),
        ),
        out_specs=P("req", "tp"),
        check_vma=False,
    )
```

```python
import functools

import jax
import jax.numpy as jnp
from jax import lax
from jax.experimental import pallas as pl
from jax.experimental.pallas import tpu as pltpu
from jax.sharding import PartitionSpec as P

ADAPTER_SCALE = 0.5
X, CORES = 4, 2
LANES = X * CORES
ORDER = (4, 5, 2, 6, 3, 7, 1)
BOTH = ("req", "tp")


def lane_shift(groups, dx, dc):
    return [
        (g * LANES + x * CORES + c, g * LANES + (x + dx) % X * CORES + (c + dc) % CORES)
        for g in range(groups)
        for x in range(X)
        for c in range(CORES)
    ]


def relative(lane, other):
    dx = (lane // CORES - other // CORES) % X
    dc = (lane % CORES - other % CORES) % CORES
    return dx * CORES + dc


VMEM = pl.BlockSpec(memory_space=pltpu.VMEM)
SMEM = pl.BlockSpec(memory_space=pltpu.SMEM)
ANY = pl.BlockSpec(memory_space=pl.ANY)


def reached(lane, k):
    return (lane // CORES + k // CORES) % X * CORES + (lane % CORES + k % CORES) % CORES


def split_down_kernel(lane_ref, down_ref, *outs):
    for k in range(LANES):
        outs[k][...] = down_ref[reached(lane_ref[0], k)]


def split_up_kernel(lane_ref, up_ref, same_ref, cross_ref):
    width = same_ref.shape[2]
    for dx in range(X):
        for dc, out_ref in enumerate((same_ref, cross_ref)):
            col = pl.multiple_of(reached(lane_ref[0], dx * CORES + dc) * width, width)
            out_ref[dx] = up_ref[0, :, pl.ds(col, width)]


def split_up(lane, up):
    rank, cols = up.shape[1:]
    return pl.pallas_call(
        split_up_kernel,
        in_specs=[SMEM, VMEM],
        out_specs=[VMEM, VMEM],
        out_shape=[jax.ShapeDtypeStruct((X, rank, cols // LANES), up.dtype)] * CORES,
        compiler_params=pltpu.CompilerParams(vmem_limit_bytes=16 * 2**20),
        name="split_up",
    )(lane, up)


def pair_kernel(same_ref, cross_ref, *outs):
    for dx in range(X):
        outs[dx][0] = same_ref[dx]
        outs[dx][1] = cross_ref[dx]


def pair_up(same, cross):
    shape = (CORES,) + same.shape[1:]
    return pl.pallas_call(
        pair_kernel,
        in_specs=[VMEM, VMEM],
        out_specs=[VMEM] * X,
        out_shape=[jax.ShapeDtypeStruct(shape, same.dtype)] * X,
        compiler_params=pltpu.CompilerParams(vmem_limit_bytes=16 * 2**20),
        name="pair_up",
    )(same, cross)


def pick_up_kernel(pick_ref, *rest):
    srcs, out_ref, staged = rest[:X], rest[X], rest[X + 1]
    for dx in range(X):
        for dc in range(CORES):
            staged[dx * CORES + dc] = srcs[dx][dc]
    for g in range(out_ref.shape[0]):
        out_ref[g] = staged[pick_ref[g]]


def pick_up(shifts, pairs):
    groups = shifts.shape[0]
    shape, dtype = pairs[0].shape[1:], pairs[0].dtype
    return pl.pallas_call(
        pick_up_kernel,
        in_specs=[SMEM] + [VMEM] * X,
        out_specs=VMEM,
        out_shape=jax.ShapeDtypeStruct((groups,) + shape, dtype),
        scratch_shapes=[pltpu.VMEM((LANES,) + shape, dtype)],
        compiler_params=pltpu.CompilerParams(vmem_limit_bytes=16 * 2**20),
        name="pick_up",
    )(shifts, *pairs)


def split(kernel, lane, whole, piece, name):
    return pl.pallas_call(
        kernel,
        in_specs=[SMEM, VMEM],
        out_specs=[VMEM] * LANES,
        out_shape=[jax.ShapeDtypeStruct(piece, whole.dtype)] * LANES,
        compiler_params=pltpu.CompilerParams(vmem_limit_bytes=16 * 2**20),
        name=name,
    )(lane, whole)


def spread(pieces, groups):
    return [
        lax.ppermute(pieces[k], BOTH, lane_shift(groups, k // CORES, k % CORES)) for k in ORDER
    ] + [pieces[0]]


def pick_kernel(pick_ref, *rest):
    srcs, out_ref, staged = rest[:LANES], rest[LANES], rest[LANES + 1]
    for src, k in zip(srcs, ORDER + (0,)):
        staged[k] = src[...]
    for g in range(out_ref.shape[0]):
        out_ref[g] = staged[pick_ref[g]]


def pick(shifts, pieces, name):
    groups = shifts.shape[0]
    shape, dtype = pieces[0].shape, pieces[0].dtype
    return pl.pallas_call(
        pick_kernel,
        in_specs=[SMEM] + [VMEM] * LANES,
        out_specs=VMEM,
        out_shape=jax.ShapeDtypeStruct((groups,) + shape, dtype),
        scratch_shapes=[pltpu.VMEM((LANES,) + shape, dtype)],
        compiler_params=pltpu.CompilerParams(vmem_limit_bytes=16 * 2**20),
        name=name,
    )(shifts, *pieces)


CHUNK = 1024
NORM_ROWS = 128


def norm_base_kernel(x_ref, gain_ref, weight_ref, normed_ref, base_ref):
    rows, features = x_ref.shape
    squares = jnp.zeros((rows, 128), jnp.float32)
    for p in range(features // 128):
        wide = x_ref[:, p * 128 : (p + 1) * 128].astype(jnp.float32)
        squares = squares + wide * wide
    mean = jnp.sum(squares, axis=1, keepdims=True) / features
    inverse_rms = lax.rsqrt(mean + 1e-05)
    total = jnp.zeros(base_ref.shape, jnp.float32)
    for p in range(features // CHUNK):
        cols = slice(p * CHUNK, (p + 1) * CHUNK)
        wide = x_ref[:, cols].astype(jnp.float32)
        normed = (wide * inverse_rms * gain_ref[:, cols]).astype(jnp.bfloat16)
        normed_ref[:, cols] = normed
        total += jnp.dot(normed, weight_ref[cols, :], preferred_element_type=jnp.float32)
    base_ref[...] = total


def norm_base(hidden, gain, weight):
    rows, features = hidden.shape
    cols = weight.shape[1]
    return pl.pallas_call(
        norm_base_kernel,
        grid=(rows // NORM_ROWS,),
        in_specs=[
            pl.BlockSpec((NORM_ROWS, features), lambda i: (i, 0)),
            pl.BlockSpec((1, features), lambda i: (0, 0)),
            pl.BlockSpec((features, cols), lambda i: (0, 0), pipeline_mode=pl.Buffered(1)),
        ],
        out_specs=[
            pl.BlockSpec((NORM_ROWS, features), lambda i: (i, 0)),
            pl.BlockSpec((NORM_ROWS, cols), lambda i: (i, 0)),
        ],
        out_shape=[
            jax.ShapeDtypeStruct((rows, features), jnp.bfloat16),
            jax.ShapeDtypeStruct((rows, cols), jnp.float32),
        ],
        compiler_params=pltpu.CompilerParams(vmem_limit_bytes=56 * 2**20),
        cost_estimate=pl.CostEstimate(
            flops=4 * rows * features * cols,
            bytes_accessed=4 * rows * features + 2 * features * cols,
            transcendentals=rows,
        ),
        name="norm_base",
    )(hidden, gain.reshape(1, features), weight)


def shrink_kernel(row_ref, down_ref, normed_hbm, low_ref, normed_ref, sems):
    blocks, block = low_ref.shape[0], low_ref.shape[2]

    def rows_of(j):
        return pl.ds(pl.multiple_of(j * block, block), block)

    def copy(j):
        return pltpu.make_async_copy(normed_hbm.at[rows_of(j)], normed_ref.at[rows_of(j)], sems.at[j])

    for j in range(blocks):
        copy(j).start()

    @pl.loop(0, blocks)
    def _(j):
        copy(j).wait()
        low_ref[j] = lax.dot_general(
            down_ref[row_ref[j]],
            normed_ref[rows_of(j), :],
            (((1,), (1,)), ((), ())),
            preferred_element_type=jnp.float32,
        )


def shrink(owner_rows, down_got, normed):
    blocks = owner_rows.shape[0]
    rows, features = normed.shape
    piece = down_got.shape[1]
    return pl.pallas_call(
        shrink_kernel,
        in_specs=[SMEM, VMEM, ANY],
        out_specs=VMEM,
        out_shape=jax.ShapeDtypeStruct((blocks, piece, rows // blocks), jnp.float32),
        scratch_shapes=[pltpu.VMEM((rows, features), jnp.bfloat16), pltpu.SemaphoreType.DMA((blocks,))],
        compiler_params=pltpu.CompilerParams(vmem_limit_bytes=48 * 2**20),
        cost_estimate=pl.CostEstimate(
            flops=2 * rows * features * 256, bytes_accessed=2 * rows * features, transcendentals=0
        ),
        name="shrink",
    )(owner_rows, down_got, normed)


def gather_kernel(lane_ref, low2, low1, low3, low0, base_hbm, low_ref, base_ref, full, sem):
    copy = pltpu.make_async_copy(base_hbm, base_ref, sem)
    copy.start()
    lows = (low0, low1, low2, low3)
    lane = lane_ref[0]
    blocks, part, _ = low0.shape[1:]
    for dx in range(X):
        for dc in range(CORES):
            src = (lane // CORES - dx) % X * CORES + (lane % CORES - dc) % CORES
            rows = pl.ds(pl.multiple_of(src * part, part), part)
            for j in range(blocks):
                full[j, rows, :] = lows[dx][dc, j]
    for j in range(blocks):
        low_ref[j] = full[j].T.astype(low_ref.dtype)
    copy.wait()


def gather_low(lane, lows, base):
    blocks, part, block = lows[0].shape[1:]
    shape = (blocks, part * LANES, block)
    return pl.pallas_call(
        gather_kernel,
        in_specs=[SMEM] + [VMEM] * len(lows) + [ANY],
        out_specs=[VMEM, VMEM],
        out_shape=[
            jax.ShapeDtypeStruct((blocks, block, part * LANES), jnp.bfloat16),
            jax.ShapeDtypeStruct(base.shape, base.dtype),
        ],
        scratch_shapes=[pltpu.VMEM(shape, jnp.float32), pltpu.SemaphoreType.DMA],
        compiler_params=pltpu.CompilerParams(vmem_limit_bytes=16 * 2**20),
        name="gather_low",
    )(lane, lows[2], lows[1], lows[3], lows[0], base)


def expand_kernel(row_ref, low_ref, base_ref, up_ref, out_hbm, out_ref, sems):
    blocks, block, _ = low_ref.shape
    copies = []
    for j in range(blocks):
        rows = pl.ds(j * block, block)
        term = jnp.dot(low_ref[j], up_ref[row_ref[j]], preferred_element_type=jnp.float32)
        out_ref[rows, :] = (base_ref[rows, :] + ADAPTER_SCALE * term).astype(out_ref.dtype)
        copies.append(pltpu.make_async_copy(out_ref.at[rows], out_hbm.at[rows], sems.at[j]))
        copies[j].start()
    for copy in copies:
        copy.wait()


def expand(owner_rows, low, base, up_got):
    return pl.pallas_call(
        expand_kernel,
        in_specs=[SMEM, VMEM, VMEM, VMEM],
        out_specs=ANY,
        out_shape=jax.ShapeDtypeStruct(base.shape, jnp.bfloat16),
        scratch_shapes=[
            pltpu.VMEM(base.shape, jnp.bfloat16),
            pltpu.SemaphoreType.DMA((low.shape[0],)),
        ],
        compiler_params=pltpu.CompilerParams(vmem_limit_bytes=16 * 2**20),
        name="expand",
    )(owner_rows, low, base, up_got)


def shards(
    hidden,
    norm_gain_vector,
    query_weight,
    adapter_down_weight,
    adapter_up_weight,
    block_adapter_ids,
    adapter_slot_table,
):
    groups, blocks = block_adapter_ids.shape
    rank, features = adapter_down_weight.shape[1:]
    lane = lax.axis_index("tp")
    group = lax.axis_index("req")
    lane_arr = lane.reshape(1).astype(jnp.int32)

    piece = (rank // LANES, features)
    down_whole = adapter_down_weight.reshape((LANES,) + piece)
    down_row = spread(split(split_down_kernel, lane_arr, down_whole, piece, "split_down"), groups)

    matches = block_adapter_ids[:, :, None] == jnp.arange(adapter_slot_table.shape[0], dtype=jnp.int32)
    slots = jnp.sum(jnp.where(matches, adapter_slot_table, 0), axis=2)
    here = slots // LANES == group
    wanted = relative(lane, jnp.sum(jnp.where(here, slots % LANES, 0), axis=1))
    owner_rows = lax.dynamic_index_in_dim(slots, group, 0, keepdims=False) // LANES

    down_send, hidden, adapter_up_weight = lax.optimization_barrier(
        (pick(wanted, down_row, "pick_down"), hidden, adapter_up_weight)
    )
    down_got = lax.all_to_all(down_send, "req", 0, 0, tiled=True)
    same, cross = split_up(lane_arr, adapter_up_weight)
    cross = lax.ppermute(cross, BOTH, lane_shift(groups, 0, 1))
    pairs = pair_up(same, cross)
    pairs = [pairs[0]] + [lax.ppermute(pairs[dx], BOTH, lane_shift(groups, dx, 0)) for dx in range(1, X)]
    normed, base = norm_base(hidden, norm_gain_vector, query_weight)
    pairs, base = lax.optimization_barrier((pairs, base))
    up_got = lax.all_to_all(pick_up(wanted, pairs), "req", 0, 0, tiled=True)

    low = shrink(owner_rows, down_got, normed)
    other = lax.ppermute(low, BOTH, lane_shift(groups, 0, 1))
    chip = jnp.stack([low, other])
    far, right, left = [lax.ppermute(chip, BOTH, lane_shift(groups, dx, 0)) for dx in (2, 1, 3)]
    lows = [chip, right, far, left]
    low, base = gather_low(lane_arr, lows, base)
    return expand(owner_rows, low, base, up_got)


def solution(mesh):
    return jax.shard_map(
        shards,
        mesh=mesh,
        in_specs=(
            P("req", None),
            P(),
            P(None, "tp"),
            P(("req", "tp"), None, None),
            P(("req", "tp"), None, None),
            P(),
            P(),
        ),
        out_specs=P("req", "tp"),
        check_vma=False,
    )
```
